256 devices in a mesh: dp: 16 (over z_hi, y), tensor: 16 (over z_lo, x, core).
Axes of the slice: x: 4, y: 4, z: 8 (z_hi: 4, z_lo: 2; z = z_hi * 2 + z_lo), core: 2. Of those that a mesh axis runs over, the one named last changes fastest.
Arguments:
- grad: bfloat16 [16, 16, 524288], P('dp', 'tensor'), may hold values from -18 to 18
- worker_err: bfloat16 [16, 16, 524288], P('dp', 'tensor'), may hold values from -3 to 3
- momentum: float32 [16, 524288], P('tensor'), may hold values from -6 to 6
- variance: float32 [16, 524288], P('tensor'), may hold values from 6e-06 to 80, as said below
- params: bfloat16 [16, 524288], P('tensor'), may hold values from -5 to 5
- server_err: float32 [16, 524288], P('tensor', 'dp'), may hold values from -3 to 3
- offsets: int32 [4], replicated, may hold values from 0 to 524160, as said below
- step_count: int32 [1], replicated, may hold values from 1 to 2000
Outputs:
- momentum_new: float32 [16, 524288], P('tensor')
- param_step: float32 [16, 524288], P('tensor')
The draws below stay inside these ranges and needn't reach their ends.
Inputs may be any that keep to these rules, and one draw needn't show every extreme that they name: offsets[0] is 0; the entries strictly increase and are multiples of 128; the last entry is 524160. `variance`: positive entries.
All inputs are finite; a program needn't handle non-finite values. Where the reference program divides by a largest or mean magnitude, that divisor is 1e-20 or more.
Results may differ from the reference program's by a relative error of at most 0.013.
Values may be sent and summed in bfloat16 or wider, within the bound.
No kernel may reach another device: no remote copies, remote signals or barrier semaphores. Data moves between devices by JAX's collectives and lax.ppermute only.
A program may use at most 64 MiB of HBM per device.

```python
import jax
import jax.numpy as jnp
from jax import lax

BUCKET = 524288
QB = 128
SEGS = 4
N_DP = 16
N_TENSOR = 16


def shared_offsets(key):
    blocks = BUCKET // QB
    inner = jax.random.permutation(key, blocks - 2)[:SEGS - 2] + 1
    inner = jnp.sort(inner).astype(jnp.int32)
    starts = jnp.concatenate([jnp.zeros((1,), jnp.int32), inner, jnp.full((1,), blocks - 1, jnp.int32)])
    return (starts * QB).astype(jnp.int32)


def draw_offsets(key, part):
    return shared_offsets(key)


def draw_variance(key, part):
    starts = shared_offsets(key)
    key = jax.random.fold_in(key, 7)
    key_kind, key_seg, key_elem = jax.random.split(key, 3)
    position = jnp.arange(BUCKET, dtype=jnp.int32)
    segment = jnp.sum((position[:, None] >= starts[None, :]).astype(jnp.int32), axis=1) - 1
    order = jax.random.permutation(key_kind, SEGS)
    is_low = order < SEGS // 2
    pick = jax.random.uniform(key_seg, (SEGS,), jnp.float32)
    high_lo = 2.0
    elem_lo = 0.5
    tensor_ratio = 9.0
    low_scale = jnp.exp(jnp.log(0.002) + pick * (jnp.log(0.01) - jnp.log(0.002)))
    high_scale = jnp.exp(jnp.log(high_lo) + pick * (jnp.log(20.0) - jnp.log(high_lo)))
    seg_scale = jnp.where(is_low, low_scale, high_scale)
    per_entry = seg_scale[segment]
    rows = jnp.arange(N_TENSOR, dtype=jnp.float32) / max(N_TENSOR - 1, 1)
    row_scale = jnp.power(tensor_ratio, -rows)
    elem = jax.random.uniform(key_elem, (N_TENSOR, BUCKET), jnp.float32)
    elem_scale = jnp.exp(jnp.log(elem_lo) + elem * (jnp.log(1.0 / elem_lo) * 2.0))
    return (per_entry[None, :] * row_scale[:, None] * elem_scale).astype(jnp.float32)


def block_levels(key, shape, cuts, smallest, high):
    loudness, own = 1.0, jax.random.fold_in(key, 6)
    for dim, shards_of in cuts:
        draws = jnp.exp(jax.random.uniform(jax.random.fold_in(own, dim), (shards_of,), jnp.float32, smallest / len(cuts), high / len(cuts)))
        loudness = loudness * jnp.repeat(draws, shape[dim] // shards_of).reshape([-1 if axis == dim else 1 for axis in range(len(shape))])
    return loudness


def centred(own_key, extent, spread, limit, cuts=(), kind=jnp.bfloat16):
    values = spread * jax.random.normal(own_key, extent, jnp.float32)
    if cuts:
        values = values * block_levels(own_key, extent, cuts, -0.22, 0.18)
    return jnp.clip(values, -limit, limit).astype(kind)


def setup_inputs(seed: int = 0) -> dict:
    streams_of = jax.random.split(jax.random.key(seed), 9)
    grad = centred(streams_of[0], (N_DP, N_TENSOR, BUCKET), 3.0, 18.0, ((0, 16), (1, 16)))
    worker_err = centred(streams_of[1], (N_DP, N_TENSOR, BUCKET), 0.5, 3.0, ((0, 16), (1, 16)))
    momentum = centred(streams_of[2], (N_TENSOR, BUCKET), 1.0, 6.0, ((0, 16),), jnp.float32)
    variance = draw_variance(jax.random.fold_in(streams_of[8], 71), 0)
    params = centred(streams_of[4], (N_TENSOR, BUCKET), 1.0, 5.0, ((0, 16),))
    server_err = centred(streams_of[5], (N_TENSOR, BUCKET), 0.5, 3.0, ((0, 16), (1, 16)), jnp.float32)
    offsets = draw_offsets(jax.random.fold_in(streams_of[8], 71), 0)
    step_count = jax.random.randint(streams_of[7], (1,), 1, 2001).astype(jnp.int32)
    return dict(grad=grad, worker_err=worker_err, momentum=momentum, variance=variance, params=params, server_err=server_err, offsets=offsets, step_count=step_count)


BETA_ONE = 0.9
BETA_TWO = 0.999
ADAM_EPS = 1e-08
DECAY = 0.1
CLIP_RMS = 2.0

def encode(values):
    scales = (lax.optimization_barrier(jnp.max(jnp.abs(values), axis=-1)) + 1e-06).astype(jnp.bfloat16)
    levels = (values / scales.astype(jnp.float32)[..., None]).astype(jnp.bfloat16)
    return (levels, scales)

def decode(levels, scales):
    return levels.astype(jnp.float32) * scales.astype(jnp.float32)[..., None]

def membership(offsets, total_blocks, first_block, count):
    starts = (offsets // QB).astype(jnp.int32)
    ends = jnp.concatenate([starts[1:], jnp.full((1,), total_blocks, jnp.int32)])
    index = (first_block + jnp.arange(count, dtype=jnp.int32)).astype(jnp.int32)
    member = ((index[None, :] >= starts[:, None]) & (index[None, :] < ends[:, None])).astype(jnp.float32)
    return (member, (ends - starts).astype(jnp.float32))

def reference(grad, worker_err, momentum, variance, params, server_err, offsets, step_count):
    blocks = BUCKET // QB

    def one_bucket(inputs):
        grads, errors, moment, spare = inputs
        worker_in = BETA_ONE * moment[None, :] + (1.0 - BETA_ONE) * grads.astype(jnp.float32) + errors.astype(jnp.float32)
        levels, scales = encode(worker_in.reshape(N_DP, blocks, QB))
        averaged = lax.optimization_barrier(jnp.sum(decode(levels, scales), axis=0)) / N_DP
        server_in = averaged + spare.reshape(blocks, QB)
        levels, scales = encode(server_in)
        return decode(levels, scales).reshape(BUCKET)
    momentum_new = lax.map(one_bucket, (jnp.swapaxes(grad, 0, 1), jnp.swapaxes(worker_err, 0, 1), momentum, server_err))
    steps = step_count[0].astype(jnp.float32)
    first = 1.0 - jnp.power(jnp.float32(BETA_ONE), steps)
    second = 1.0 - jnp.power(jnp.float32(BETA_TWO), steps)
    direction = momentum_new / first / (jnp.sqrt(variance / second) + ADAM_EPS)
    squares = lax.optimization_barrier(jnp.sum(lax.optimization_barrier(jnp.sum((direction * direction).reshape(N_TENSOR, blocks, QB), axis=2)), axis=0))
    member, counts = membership(offsets, blocks, 0, blocks)
    totals = jnp.dot(member, squares, precision=lax.Precision.HIGHEST)
    root_mean = jnp.sqrt(totals / (counts * QB * N_TENSOR) + 1e-06)
    factor = jnp.maximum(1.0, root_mean / CLIP_RMS)
    per_block = jnp.dot(factor, member, precision=lax.Precision.HIGHEST)
    shaped = direction.reshape(N_TENSOR, blocks, QB) / per_block[None, :, None]
    param_step = shaped.reshape(N_TENSOR, BUCKET) + DECAY * params.astype(jnp.float32)
    return (momentum_new, param_step)
```

```python
import jax
import jax.numpy as jnp
from jax import lax
from jax.experimental import pallas as pl
from jax.experimental.pallas import tpu as pltpu
from jax.sharding import PartitionSpec as P

QB = 128
BETA_ONE = 0.9
BETA_TWO = 0.999
ADAM_EPS = 1e-08
DECAY = 0.1
CLIP_RMS = 2.0

BUCKET = 524288
SEGS = 4
N_Z = 4
N_Y = 4
N_DP = N_Z * N_Y
N_TENSOR = 16
SHARE = BUCKET // N_DP
ROWS = SHARE // QB
BLOCKS = BUCKET // QB
F32 = jnp.float32
BF16 = jnp.bfloat16
VMEM_LIMIT = 48 * 1024 * 1024


def params_of(**kwargs):
    return pltpu.CompilerParams(vmem_limit_bytes=VMEM_LIMIT, **kwargs)


def whole(shape):
    return pl.BlockSpec(shape, lambda i, *_: (0,) * len(shape))


def rows_of(values):
    return values.reshape(values.shape[-1] // QB, QB)


def prepare_kernel(place, grad, err, *outs):
    y = place[1]
    for k in range(N_Y):
        start = pl.multiple_of((y ^ k) * SHARE, SHARE)
        g = grad[0, :, pl.ds(start, SHARE)].astype(F32)
        e = err[0, :, pl.ds(start, SHARE)].astype(F32)
        outs[k][0] = rows_of((1.0 - BETA_ONE) * g + e).astype(BF16)


def prepare(place, grad, err):
    quarter = pl.BlockSpec((1, 1, N_Y * SHARE), lambda i, *_: (0, 0, i))
    out = jax.ShapeDtypeStruct((N_Z, ROWS, QB), BF16)
    return pl.pallas_call(
        prepare_kernel,
        grid_spec=pltpu.PrefetchScalarGridSpec(
            num_scalar_prefetch=1,
            grid=(N_Z,),
            in_specs=[quarter, quarter],
            out_specs=[pl.BlockSpec((1, ROWS, QB), lambda i, *_: (i, 0, 0))] * N_Y,
        ),
        out_shape=(out,) * N_Y,
        compiler_params=params_of(),
    )(place, grad, err)


def reduce_y_kernel(place, *refs):
    ins, outs = refs[:N_Y], refs[N_Y:]
    z = place[0]
    for k in range(N_Z):
        total = ins[0][z ^ k].astype(F32)
        for ref in ins[1:]:
            total = total + ref[z ^ k].astype(F32)
        outs[k][...] = total.astype(BF16)


def reduce_y(place, pieces):
    out = jax.ShapeDtypeStruct((ROWS, QB), BF16)
    return pl.pallas_call(
        reduce_y_kernel,
        grid_spec=pltpu.PrefetchScalarGridSpec(
            num_scalar_prefetch=1,
            grid=(1,),
            in_specs=[whole((N_Z, ROWS, QB))] * N_Y,
            out_specs=[whole((ROWS, QB))] * N_Z,
        ),
        out_shape=(out,) * N_Z,
        compiler_params=params_of(),
    )(place, *pieces)


def row_masks(starts, first_row, rows):
    index = first_row + lax.broadcasted_iota(jnp.int32, (rows, QB), 0)
    return [index >= starts[k] for k in range(1, SEGS)]


def server_kernel(place, starts, bias, *refs):
    ins = refs[:N_Z]
    momentum, variance, server_err, out = refs[N_Z:]
    total = ins[0][...].astype(F32)
    for ref in ins[1:]:
        total = total + ref[...].astype(F32)
    value = total * (1.0 / N_DP) + BETA_ONE * rows_of(momentum[...]) + rows_of(server_err[...])
    sent = value.astype(BF16)
    out[:ROWS, :] = sent
    kept = sent.astype(F32)
    direction = kept * bias[0] / (jnp.sqrt(rows_of(variance[...]) * bias[1]) + ADAM_EPS)
    squares = direction * direction
    masks = row_masks(starts, (place[0] * N_Y + place[1]) * ROWS, ROWS)
    seg = []
    for k in range(SEGS):
        picked = squares
        if k > 0:
            picked = jnp.where(masks[k - 1], picked, 0.0)
        if k < SEGS - 1:
            picked = jnp.where(masks[k], 0.0, picked)
        seg.append(jnp.sum(picked, axis=0, keepdims=True))
    sums = jnp.concatenate(seg + [jnp.zeros((8 - SEGS, QB), F32)], axis=0)
    high = sums.astype(BF16).astype(F32)
    low = sums - high
    out[ROWS:, :] = jnp.concatenate([high, low], axis=0).astype(BF16)


def server(place, starts, bias, pieces, momentum, variance, server_err):
    mine = pl.BlockSpec((1, SHARE), lambda i, place, *_: (0, place[0] * N_Y + place[1]))
    return pl.pallas_call(
        server_kernel,
        grid_spec=pltpu.PrefetchScalarGridSpec(
            num_scalar_prefetch=3,
            grid=(1,),
            in_specs=[whole((ROWS, QB))] * N_Z + [mine, mine, whole((1, SHARE))],
            out_specs=whole((ROWS + 16, QB)),
        ),
        out_shape=jax.ShapeDtypeStruct((ROWS + 16, QB), BF16),
        compiler_params=params_of(),
    )(place, starts, bias, *pieces, momentum, variance, server_err)


def join_kernel(*refs):
    ins, (out, sums) = refs[:N_Z], refs[N_Z:]
    total = jnp.zeros((8, QB), F32)
    for k, ref in enumerate(ins):
        out[k] = ref[:ROWS, :]
        tail = ref[ROWS:, :].astype(F32)
        total = total + (tail[:8] + tail[8:])
    sums[...] = jnp.broadcast_to(total[None], sums.shape)


def join(pieces):
    return pl.pallas_call(
        join_kernel,
        grid=(1,),
        in_specs=[whole((ROWS + 16, QB))] * N_Z,
        out_specs=[whole((N_Z, ROWS, QB)), whole((N_TENSOR, 8, QB))],
        out_shape=(
            jax.ShapeDtypeStruct((N_Z, ROWS, QB), BF16),
            jax.ShapeDtypeStruct((N_TENSOR, 8, QB), F32),
        ),
        compiler_params=params_of(),
    )(*pieces)


def final_kernel(place, starts, bias, *refs):
    pieces = refs[:N_Y]
    totals = refs[N_Y : 2 * N_Y]
    variance, weights, momentum_out, step_out = refs[2 * N_Y :]
    z, y = place[0], place[1]
    part = pl.program_id(0)
    total = totals[0][...]
    for ref in totals[1:]:
        total = total + ref[...]
    total = jnp.sum(total, axis=1, keepdims=True)
    inverse = []
    for k in range(SEGS):
        end = starts[k + 1] if k + 1 < SEGS else BLOCKS
        entries = (end - starts[k]).astype(F32) * (QB * N_TENSOR)
        root_mean = jnp.sqrt(total[k : k + 1] / entries + 1e-06)
        inverse.append(1.0 / jnp.maximum(1.0, root_mean / CLIP_RMS))
    for k in range(N_Y):
        row = pl.multiple_of((y ^ k) * ROWS, ROWS)
        col = pl.multiple_of((y ^ k) * SHARE, SHARE)
        kept = pieces[k][part ^ z].astype(F32)
        momentum_out[pl.ds(row, ROWS), :] = kept
        spread = jnp.sqrt(rows_of(variance[:, pl.ds(col, SHARE)]) * bias[1]) + ADAM_EPS
        direction = kept * bias[0] / spread
        factor = jnp.broadcast_to(inverse[0], (ROWS, QB))
        for seg, mask in enumerate(row_masks(starts, part * (N_Y * ROWS) + row, ROWS)):
            factor = jnp.where(mask, inverse[seg + 1], factor)
        decayed = DECAY * rows_of(weights[:, pl.ds(col, SHARE)].astype(F32))
        step_out[pl.ds(row, ROWS), :] = direction * factor + decayed


def final(place, starts, bias, pieces, totals, variance, weights):
    quarter = pl.BlockSpec((1, N_Y * SHARE), lambda i, *_: (0, i))
    out = jax.ShapeDtypeStruct((BLOCKS, QB), F32)
    return pl.pallas_call(
        final_kernel,
        grid_spec=pltpu.PrefetchScalarGridSpec(
            num_scalar_prefetch=3,
            grid=(N_Z,),
            in_specs=[whole((N_Z, ROWS, QB))] * N_Y + [whole((8, QB))] * N_Y + [quarter, quarter],
            out_specs=[pl.BlockSpec((N_Y * ROWS, QB), lambda i, *_: (i, 0))] * 2,
        ),
        out_shape=(out, out),
        compiler_params=params_of(),
    )(place, starts, bias, *pieces, *totals, variance, weights)


def exchange(value, mask):
    return lax.ppermute(value, "dp", [(i, i ^ mask) for i in range(N_DP)])


def body(grad, worker_err, momentum, variance, params, server_err, offsets, step_count):
    me = lax.axis_index("dp")
    place = jnp.stack([me // N_Y, me % N_Y]).astype(jnp.int32)
    starts = (offsets // QB).astype(jnp.int32)
    steps = step_count[0].astype(F32)
    first = 1.0 - jnp.power(F32(BETA_ONE), steps)
    second = 1.0 - jnp.power(F32(BETA_TWO), steps)
    bias = jnp.stack([1.0 / first, 1.0 / second])

    to_y = prepare(place, grad, worker_err)
    pieces = [to_y[0]] + [exchange(to_y[k], k) for k in range(1, N_Y)]
    to_z = reduce_y(place, pieces)
    pieces = [to_z[0]] + [exchange(to_z[k], k * N_Y) for k in range(1, N_Z)]
    mine = server(place, starts, bias, pieces, momentum, variance, server_err)
    column, sums = join([mine] + [exchange(mine, k * N_Y) for k in range(1, N_Z)])
    columns = [column] + [exchange(column, k) for k in range(1, N_Y)]
    sums = jnp.sum(lax.all_to_all(sums, "tensor", split_axis=0, concat_axis=0, tiled=True), axis=0)
    totals = [sums] + [exchange(sums, k) for k in range(1, N_Y)]
    momentum_new, param_step = final(place, starts, bias, columns, totals, variance, params)
    return (momentum_new.reshape(1, BUCKET), param_step.reshape(1, BUCKET))


def solution(mesh):
    placed = (
        P("dp", "tensor", None),
        P("dp", "tensor", None),
        P("tensor", None),
        P("tensor", None),
        P("tensor", None),
        P("tensor", "dp"),
        P(),
        P(),
    )
    return jax.shard_map(
        body,
        mesh=mesh,
        in_specs=placed,
        out_specs=(P("tensor", None), P("tensor", None)),
        check_vma=False,
    )
```

```python
import jax
import jax.numpy as jnp
from jax import lax
from jax.experimental import pallas as pl
from jax.experimental.pallas import tpu as pltpu
from jax.sharding import Mesh, PartitionSpec as P

QB = 128
BETA_ONE = 0.9
BETA_TWO = 0.999
ADAM_EPS = 1e-08
DECAY = 0.1
CLIP_RMS = 2.0

BUCKET = 524288
SEGS = 4
N_Z = 4
N_Y = 4
N_DP = N_Z * N_Y
N_TENSOR = 16
SHARE = BUCKET // N_DP
ROWS = SHARE // QB
BLOCKS = BUCKET // QB
HALF = N_Z // 2
F32 = jnp.float32
BF16 = jnp.bfloat16
MIB = 1024 * 1024
PREPARE_LIMIT = 60
STEP_ROWS = 512
ORDER = (2, 1, 3)
LAST_ORDER = (3, 1, 2)


def on_chip(count):
    return [pl.BlockSpec(memory_space=pltpu.VMEM)] * count


def anywhere(count):
    return [pl.BlockSpec(memory_space=pl.ANY)] * count


def like(shape, dtype):
    return jax.ShapeDtypeStruct(shape, dtype)


def rows_of(values):
    return values.reshape(values.shape[-1] // QB, QB)


def call(kernel, scalars, arrays, in_specs, out_specs, out_shape, scratch=(), limit=16):
    return pl.pallas_call(
        kernel,
        in_specs=[pl.BlockSpec(memory_space=pltpu.SMEM)] * len(scalars) + in_specs,
        out_specs=out_specs,
        out_shape=out_shape,
        scratch_shapes=scratch,
        compiler_params=pltpu.CompilerParams(vmem_limit_bytes=limit * MIB),
    )(*scalars, *arrays)


def my_z():
    return lax.axis_index("z")


def my_y():
    return lax.axis_index("y")


def share_of(ref, block):
    return rows_of(ref[:, pl.ds(pl.multiple_of(block * SHARE, SHARE), SHARE)])


def rows_at(block):
    return pl.ds(pl.multiple_of(block * ROWS, ROWS), ROWS)


def prepare_kernel(grad, err, *refs):
    outs, (held_grad, held_err, sems) = refs[:N_Y], refs[N_Y:]
    y = my_y()
    copies = []
    for s in range(N_Z):
        block = pl.ds(s * N_Y * SHARE, N_Y * SHARE)
        copies.append(
            (
                pltpu.make_async_copy(grad.at[:, :, block], held_grad.at[:, :, block], sems.at[0, s]),
                pltpu.make_async_copy(err.at[:, :, block], held_err.at[:, :, block], sems.at[1, s]),
            )
        )
    for pair in copies:
        for copy in pair:
            copy.start()
    for s in range(N_Z):
        for copy in copies[s]:
            copy.wait()
        for k in range(N_Y):
            block = pl.ds(pl.multiple_of((s * N_Y + (y ^ k)) * SHARE, SHARE), SHARE)
            g = held_grad[0, :, block].astype(F32)
            e = held_err[0, :, block].astype(F32)
            outs[k][s] = rows_of((1.0 - BETA_ONE) * g + e).astype(BF16)


def prepare(grad, err):
    held = pltpu.VMEM((1, 1, BUCKET), BF16)
    return call(
        prepare_kernel,
        (),
        (grad, err),
        anywhere(2),
        on_chip(N_Y),
        (like((N_Z, ROWS, QB), BF16),) * N_Y,
        scratch=[held, held, pltpu.SemaphoreType.DMA((2, N_Z))],
        limit=PREPARE_LIMIT,
    )


def reduce_y_kernel(*refs):
    ins, server_err, outs = refs[:N_Y], refs[N_Y], refs[-2:]
    mine = rows_of(server_err[...])
    z = my_z()
    for s in range(N_Z):
        total = ins[0][s].astype(F32)
        for ref in ins[1:]:
            total = total + ref[s].astype(F32)
        total = total * (1.0 / N_DP) + jnp.where(z == s, mine, 0.0)
        outs[s // HALF][s % HALF] = total.astype(BF16)


def reduce_y(pieces, server_err, *staged):
    return call(
        reduce_y_kernel,
        (),
        (*pieces, server_err, *staged),
        on_chip(N_Y + 1) + anywhere(len(staged)),
        on_chip(2),
        (like((HALF, ROWS, QB), BF16),) * 2,
    )


def add_kernel(ours, theirs, out):
    out[...] = (ours[...].astype(F32) + theirs[...].astype(F32)).astype(BF16)


def add(ours, theirs):
    (out,) = call(add_kernel, (), (ours, theirs), on_chip(2), on_chip(1), [like((HALF, ROWS, QB), BF16)])
    return out


def row_masks(offsets, first_row, rows):
    entry = (first_row + lax.broadcasted_iota(jnp.int32, (rows, QB), 0)) * QB
    return [entry >= offsets[k] for k in range(1, SEGS)]


def server_kernel(offsets, low, high, other_low, other_high, momentum, spread, column, out):
    y = my_y()
    seg = [jnp.zeros((1, QB), F32)] * SEGS
    for s in range(N_Z):
        ours, theirs = (low, other_low) if s < HALF else (high, other_high)
        total = ours[s % HALF].astype(F32) + theirs[s % HALF].astype(F32)
        block = s * N_Y + y
        sent = (total + BETA_ONE * share_of(momentum, block)).astype(BF16)
        column[s] = sent
        direction = sent.astype(F32) * spread[s]
        squares = direction * direction
        masks = row_masks(offsets, block * ROWS, ROWS)
        for k in range(SEGS):
            picked = squares
            if k > 0:
                picked = jnp.where(masks[k - 1], picked, 0.0)
            if k < SEGS - 1:
                picked = jnp.where(masks[k], 0.0, picked)
            seg[k] = seg[k] + jnp.sum(picked, axis=0, keepdims=True)
    sums = jnp.concatenate(seg + [jnp.zeros((8 - SEGS, QB), F32)], axis=0)
    sums = sums + pltpu.roll(sums, QB // 2, 1)
    sums = sums + pltpu.roll(sums, QB // 4, 1)
    lane = lax.broadcasted_iota(jnp.int32, (8, QB), 1) // (QB // SEGS)
    mine = jnp.where(lane == lax.broadcasted_iota(jnp.int32, (8, QB), 0), sums, 0.0)
    out[...] = jnp.broadcast_to(jnp.sum(mine, axis=0, keepdims=True)[None], out.shape)


def server(offsets, halves, momentum, spread):
    return call(
        server_kernel,
        (offsets,),
        (*halves, momentum, spread),
        on_chip(6),
        on_chip(2),
        (like((N_Z, ROWS, QB), BF16), like((N_Y * N_TENSOR, 1, QB), F32)),
    )


def stage_kernel(bias, variance, weights, spread, column_spread, dense, held, sems):
    copies = []
    for block in range(N_DP):
        rows = pl.ds(block * ROWS, ROWS)
        root = jnp.sqrt(share_of(variance, block) * bias[1]) + ADAM_EPS
        held[rows, :] = bias[0] / root
        dense[rows, :] = share_of(weights, block).astype(BF16)
        if block % N_Y == N_Y - 1:
            rows = pl.ds((block + 1 - N_Y) * ROWS, N_Y * ROWS)
            copies.append(pltpu.make_async_copy(held.at[rows], spread.at[rows], sems.at[block // N_Y]))
            copies[-1].start()
    for s in range(N_Z):
        column_spread[s] = held[rows_at(s * N_Y + my_y()), :]
    for copy in copies:
        copy.wait()


def stage(bias, variance, weights):
    return call(
        stage_kernel,
        (bias,),
        (variance, weights),
        on_chip(2),
        anywhere(1) + on_chip(2),
        (like((BLOCKS, QB), F32), like((N_Z, ROWS, QB), F32), like((BLOCKS, QB), BF16)),
        scratch=[pltpu.VMEM((BLOCKS, QB), F32), pltpu.SemaphoreType.DMA((N_Z,))],
    )


def momentum_kernel(*refs):
    pieces, (spread, out, direction, held, held_spread, sems) = refs[:N_Y], refs[N_Y:]
    y = my_y()
    parts = [pl.ds(s * N_Y * ROWS, N_Y * ROWS) for s in range(N_Z)]
    loads = [pltpu.make_async_copy(spread.at[rows], held_spread.at[rows], sems.at[0, s]) for s, rows in enumerate(parts)]
    stores = [pltpu.make_async_copy(held.at[rows], out.at[rows], sems.at[1, s]) for s, rows in enumerate(parts)]
    for load in loads:
        load.start()
    for s in range(N_Z):
        loads[s].wait()
        for k, piece in zip((0, *LAST_ORDER), pieces):
            rows = rows_at(s * N_Y + (y ^ k))
            kept = piece[s].astype(F32)
            held[rows, :] = kept
            direction[rows, :] = (kept * held_spread[rows, :]).astype(BF16)
        stores[s].start()
    for store in stores:
        store.wait()


def momentum_of(pieces, spread):
    held = pltpu.VMEM((BLOCKS, QB), F32)
    return call(
        momentum_kernel,
        (),
        (*pieces, spread),
        on_chip(N_Y) + anywhere(1),
        anywhere(1) + on_chip(1),
        (like((BLOCKS, QB), F32), like((BLOCKS, QB), BF16)),
        scratch=[held, held, pltpu.SemaphoreType.DMA((2, N_Z))],
    )


def step_kernel(offsets, totals, direction, dense, out, held, sems):
    total = jnp.sum(totals[...], axis=0)
    lane = lax.broadcasted_iota(jnp.int32, (1, QB), 1) // (QB // SEGS)
    inverse = []
    for k in range(SEGS):
        end = offsets[k + 1] if k + 1 < SEGS else BUCKET
        entries = (end - offsets[k]).astype(F32) * N_TENSOR
        squares = jnp.sum(jnp.where(lane == k, total, 0.0), axis=1, keepdims=True)
        inverse.append(1.0 / jnp.maximum(1.0, jnp.sqrt(squares / entries + 1e-06) / CLIP_RMS))
    count = STEP_ROWS
    copies = []
    for part in range(BLOCKS // count):
        rows = pl.ds(part * count, count)
        factor = jnp.broadcast_to(inverse[0], (count, QB))
        for seg, mask in enumerate(row_masks(offsets, part * count, count)):
            factor = jnp.where(mask, inverse[seg + 1], factor)
        held[rows, :] = direction[rows, :].astype(F32) * factor + DECAY * dense[rows, :].astype(F32)
        copies.append(pltpu.make_async_copy(held.at[rows], out.at[rows], sems.at[part]))
        copies[-1].start()
    for copy in copies:
        copy.wait()


def step_of(offsets, totals, direction, dense):
    (out,) = call(
        step_kernel,
        (offsets,),
        (totals, direction, dense),
        on_chip(3),
        anywhere(1),
        [like((BLOCKS, QB), F32)],
        scratch=[pltpu.VMEM((BLOCKS, QB), F32), pltpu.SemaphoreType.DMA((BLOCKS // STEP_ROWS,))],
    )
    return out


def exchange(value, axis, mask):
    return lax.ppermute(value, axis, [(i, i ^ mask) for i in range(lax.axis_size(axis))])


def body(grad, worker_err, momentum, variance, params, server_err, offsets, step_count):
    steps = step_count[0].astype(F32)
    first = 1.0 - jnp.power(F32(BETA_ONE), steps)
    second = 1.0 - jnp.power(F32(BETA_TWO), steps)
    bias = jnp.stack([1.0 / first, 1.0 / second])

    to_y = prepare(grad, worker_err)
    pieces = [to_y[0]] + [exchange(to_y[k], "y", k) for k in ORDER]
    spread, column_spread, dense = stage(bias, variance, params)
    low, high = reduce_y(pieces, server_err, column_spread)
    low, high = add(low, exchange(low, "z", 1)), add(high, exchange(high, "z", 3))
    halves = (low, high, exchange(low, "z", 3), exchange(high, "z", 1))
    column, squares = server(offsets, halves, momentum, column_spread)
    columns = [column] + [exchange(column, "y", k) for k in LAST_ORDER]
    totals = lax.all_to_all(squares, ("y", "tensor"), split_axis=0, concat_axis=0, tiled=True)
    momentum_new, direction = momentum_of(columns, spread)
    param_step = step_of(offsets, totals, direction, dense)
    return (momentum_new.reshape(1, BUCKET), param_step.reshape(1, BUCKET))


def solution(mesh):
    split = Mesh(mesh.devices.reshape(N_Z, N_Y, N_TENSOR), ("z", "y", "tensor"))
    dp = ("z", "y")
    placed = (
        P(dp, "tensor", None),
        P(dp, "tensor", None),
        P("tensor", None),
        P("tensor", None),
        P("tensor", None),
        P("tensor", dp),
        P(),
        P(),
    )
    return jax.shard_map(
        body,
        mesh=split,
        in_specs=placed,
        out_specs=(P("tensor", None), P("tensor", None)),
        check_vma=False,
    )
```

```python
import functools

import jax
import jax.numpy as jnp
from jax import lax
from jax.experimental import pallas as pl
from jax.experimental.pallas import tpu as pltpu
from jax.sharding import Mesh, PartitionSpec as P

QB = 128
BETA_ONE = 0.9
BETA_TWO = 0.999
ADAM_EPS = 1e-08
DECAY = 0.1
CLIP_RMS = 2.0

BUCKET = 524288
SEGS = 4
N_Z = 4
N_Y = 4
N_DP = N_Z * N_Y
N_TENSOR = 16
SHARE = BUCKET // N_DP
ROWS = SHARE // QB
BLOCKS = BUCKET // QB
HALF = N_Z // 2
HALF_SHAPE = (HALF, ROWS, QB)
F32 = jnp.float32
BF16 = jnp.bfloat16
MIB = 1024 * 1024
PREPARE_LIMIT = 60
STEP_ROWS = 512
ORDER = (2, 1, 3)
LAST_ORDER = (3, 1, 2)


def on_chip(count):
    return [pl.BlockSpec(memory_space=pltpu.VMEM)] * count


def anywhere(count):
    return [pl.BlockSpec(memory_space=pl.ANY)] * count


def like(shape, dtype):
    return jax.ShapeDtypeStruct(shape, dtype)


def rows_of(values):
    return values.reshape(values.shape[-1] // QB, QB)


def call(kernel, scalars, arrays, in_specs, out_specs, out_shape, scratch=(), limit=16, aliases=None):
    return pl.pallas_call(
        kernel,
        in_specs=[pl.BlockSpec(memory_space=pltpu.SMEM)] * len(scalars) + in_specs,
        out_specs=out_specs,
        out_shape=out_shape,
        scratch_shapes=scratch,
        input_output_aliases=aliases or {},
        compiler_params=pltpu.CompilerParams(vmem_limit_bytes=limit * MIB),
    )(*scalars, *arrays)


def my_z():
    return lax.axis_index("z")


def my_y():
    return lax.axis_index("y")


def share_of(ref, block):
    return rows_of(ref[:, pl.ds(pl.multiple_of(block * SHARE, SHARE), SHARE)])


def rows_at(block):
    return pl.ds(pl.multiple_of(block * ROWS, ROWS), ROWS)


def prepare_kernel(half, grad, err, *refs):
    outs, (held_grad, held_err, sems) = refs[:N_Y], refs[N_Y:]
    y = my_y()
    width = N_Y * SHARE
    copies = []
    for s in range(HALF):
        here = pl.ds((half * HALF + s) * width, width)
        there = pl.ds(s * width, width)
        copies.append(
            (
                pltpu.make_async_copy(grad.at[:, :, here], held_grad.at[:, :, there], sems.at[0, s]),
                pltpu.make_async_copy(err.at[:, :, here], held_err.at[:, :, there], sems.at[1, s]),
            )
        )
    for pair in copies:
        for copy in pair:
            copy.start()
    for s in range(HALF):
        for copy in copies[s]:
            copy.wait()
        for k in range(N_Y):
            block = pl.ds(pl.multiple_of((s * N_Y + (y ^ k)) * SHARE, SHARE), SHARE)
            g = held_grad[0, :, block].astype(F32)
            e = held_err[0, :, block].astype(F32)
            outs[k][s] = rows_of((1.0 - BETA_ONE) * g + e).astype(BF16)


def prepare(half, grad, err):
    held = pltpu.VMEM((1, 1, BUCKET // 2), BF16)
    return call(
        functools.partial(prepare_kernel, half),
        (),
        (grad, err),
        anywhere(2),
        on_chip(N_Y),
        (like(HALF_SHAPE, BF16),) * N_Y,
        scratch=[held, held, pltpu.SemaphoreType.DMA((2, HALF))],
        limit=PREPARE_LIMIT,
    )


def reduce_y_kernel(half, *refs):
    ins, server_err, out = refs[:N_Y], refs[N_Y], refs[-1]
    mine = rows_of(server_err[...])
    z = my_z()
    for s in range(HALF):
        total = ins[0][s].astype(F32)
        for ref in ins[1:]:
            total = total + ref[s].astype(F32)
        total = total * (1.0 / N_DP) + jnp.where(z == half * HALF + s, mine, 0.0)
        out[s] = total.astype(BF16)


def reduce_y(half, pieces, server_err, *staged):
    (out,) = call(
        functools.partial(reduce_y_kernel, half),
        (),
        (*pieces, server_err, *staged),
        on_chip(N_Y + 1) + anywhere(len(staged)),
        on_chip(1),
        [like(HALF_SHAPE, BF16)],
    )
    return out


def add_kernel(ours, theirs, *refs):
    out = refs[-1]
    out[...] = (ours[...].astype(F32) + theirs[...].astype(F32)).astype(BF16)


def add(ours, theirs, *staged):
    (out,) = call(
        add_kernel,
        (),
        (ours, theirs, *staged),
        on_chip(2) + anywhere(len(staged)),
        on_chip(1),
        [like(HALF_SHAPE, BF16)],
    )
    return out


def row_masks(offsets, first_row, rows):
    entry = (first_row + lax.broadcasted_iota(jnp.int32, (rows, QB), 0)) * QB
    return [entry >= offsets[k] for k in range(1, SEGS)]


def server_kernel(offsets, low, high, other_low, other_high, momentum, spread, column, out):
    y = my_y()
    seg = [jnp.zeros((1, QB), F32)] * SEGS
    for s in range(N_Z):
        ours, theirs = (low, other_low) if s < HALF else (high, other_high)
        total = ours[s % HALF].astype(F32) + theirs[s % HALF].astype(F32)
        block = s * N_Y + y
        sent = (total + BETA_ONE * share_of(momentum, block)).astype(BF16)
        column[s] = sent
        direction = sent.astype(F32) * spread[s]
        squares = direction * direction
        masks = row_masks(offsets, block * ROWS, ROWS)
        for k in range(SEGS):
            picked = squares
            if k > 0:
                picked = jnp.where(masks[k - 1], picked, 0.0)
            if k < SEGS - 1:
                picked = jnp.where(masks[k], 0.0, picked)
            seg[k] = seg[k] + jnp.sum(picked, axis=0, keepdims=True)
    sums = jnp.concatenate(seg + [jnp.zeros((8 - SEGS, QB), F32)], axis=0)
    sums = sums + pltpu.roll(sums, QB // 2, 1)
    sums = sums + pltpu.roll(sums, QB // 4, 1)
    lane = lax.broadcasted_iota(jnp.int32, (8, QB), 1) // (QB // SEGS)
    mine = jnp.where(lane == lax.broadcasted_iota(jnp.int32, (8, QB), 0), sums, 0.0)
    out[...] = jnp.broadcast_to(jnp.sum(mine, axis=0, keepdims=True)[None], out.shape)


def server(offsets, halves, momentum, spread):
    return call(
        server_kernel,
        (offsets,),
        (*halves, momentum, spread),
        on_chip(6),
        on_chip(2),
        (like((N_Z, ROWS, QB), BF16), like((N_Y * N_TENSOR, 1, QB), F32)),
    )


def spread_kernel(bias, variance, spread, column_spread):
    for block in range(N_DP):
        root = jnp.sqrt(share_of(variance, block) * bias[1]) + ADAM_EPS
        spread[block * ROWS : (block + 1) * ROWS, :] = bias[0] / root
    for s in range(N_Z):
        column_spread[s] = spread[rows_at(s * N_Y + my_y()), :]


def spread_of(bias, variance):
    return call(
        spread_kernel,
        (bias,),
        (variance,),
        on_chip(1),
        on_chip(2),
        (like((BLOCKS, QB), F32), like((N_Z, ROWS, QB), F32)),
    )


def dense_kernel(weights, out):
    for block in range(N_DP):
        out[block * ROWS : (block + 1) * ROWS, :] = share_of(weights, block).astype(BF16)


def dense_of(weights):
    (out,) = call(dense_kernel, (), (weights,), on_chip(1), on_chip(1), [like((BLOCKS, QB), BF16)])
    return out


def momentum_kernel(*refs):
    pieces, (spread, out, direction, held, sems) = refs[:N_Y], refs[N_Y:]
    y = my_y()
    stores = []
    for s in range(N_Z):
        for k, piece in zip((0, *LAST_ORDER), pieces):
            rows = rows_at(s * N_Y + (y ^ k))
            kept = piece[s].astype(F32)
            held[rows, :] = kept
            direction[rows, :] = kept * spread[rows, :]
        rows = pl.ds(s * N_Y * ROWS, N_Y * ROWS)
        stores.append(pltpu.make_async_copy(held.at[rows], out.at[rows], sems.at[s]))
        stores[-1].start()
    for store in stores:
        store.wait()


def momentum_of(pieces, spread):
    out = like((BLOCKS, QB), F32)
    return call(
        momentum_kernel,
        (),
        (*pieces, spread),
        on_chip(N_Y + 1),
        anywhere(1) + on_chip(1),
        (out, out),
        scratch=[pltpu.VMEM((BLOCKS, QB), F32), pltpu.SemaphoreType.DMA((N_Z,))],
        aliases={N_Y: 1},
    )


def step_kernel(offsets, totals, direction, dense, out, held, sems):
    total = jnp.sum(totals[...], axis=0)
    lane = lax.broadcasted_iota(jnp.int32, (1, QB), 1) // (QB // SEGS)
    inverse = []
    for k in range(SEGS):
        end = offsets[k + 1] if k + 1 < SEGS else BUCKET
        entries = (end - offsets[k]).astype(F32) * N_TENSOR
        squares = jnp.sum(jnp.where(lane == k, total, 0.0), axis=1, keepdims=True)
        inverse.append(1.0 / jnp.maximum(1.0, jnp.sqrt(squares / entries + 1e-06) / CLIP_RMS))
    count = STEP_ROWS
    copies = []
    for part in range(BLOCKS // count):
        rows = pl.ds(part * count, count)
        factor = jnp.broadcast_to(inverse[0], (count, QB))
        for seg, mask in enumerate(row_masks(offsets, part * count, count)):
            factor = jnp.where(mask, inverse[seg + 1], factor)
        held[rows, :] = direction[rows, :] * factor + DECAY * dense[rows, :].astype(F32)
        copies.append(pltpu.make_async_copy(held.at[rows], out.at[rows], sems.at[part]))
        copies[-1].start()
    for copy in copies:
        copy.wait()


def step_of(offsets, totals, direction, dense):
    (out,) = call(
        step_kernel,
        (offsets,),
        (totals, direction, dense),
        on_chip(3),
        anywhere(1),
        [like((BLOCKS, QB), F32)],
        scratch=[pltpu.VMEM((BLOCKS, QB), F32), pltpu.SemaphoreType.DMA((BLOCKS // STEP_ROWS,))],
    )
    return out


def exchange(value, axis, mask):
    return lax.ppermute(value, axis, [(i, i ^ mask) for i in range(lax.axis_size(axis))])


def exchange_z(value, even, odd):
    pairs = [
        (z * N_TENSOR + t, (z ^ (odd if t % 2 else even)) * N_TENSOR + t)
        for z in range(N_Z)
        for t in range(N_TENSOR)
    ]
    return lax.ppermute(value, ("z", "tensor"), pairs)


def body(grad, worker_err, momentum, variance, params, server_err, offsets, step_count):
    steps = step_count[0].astype(F32)
    first = 1.0 - jnp.power(F32(BETA_ONE), steps)
    second = 1.0 - jnp.power(F32(BETA_TWO), steps)
    bias = jnp.stack([1.0 / first, 1.0 / second])

    spread, column_spread = spread_of(bias, variance)
    dense = dense_of(params)
    low_y, high_y = prepare(0, grad, worker_err), prepare(1, grad, worker_err)
    low = [low_y[0]] + [exchange(low_y[k], "y", k) for k in ORDER]
    high = [high_y[0]] + [exchange(high_y[k], "y", k) for k in ORDER]
    low = reduce_y(0, low, server_err)
    high = reduce_y(1, high, server_err, dense)
    low = add(low, exchange_z(low, 1, 3))
    high = add(high, exchange_z(high, 1, 3), column_spread)
    halves = (low, high, exchange_z(low, 3, 1), exchange_z(high, 3, 1))
    column, squares = server(offsets, halves, momentum, column_spread)
    columns = [column] + [exchange(column, "y", k) for k in LAST_ORDER]
    totals = lax.all_to_all(squares, ("y", "tensor"), split_axis=0, concat_axis=0, tiled=True)
    momentum_new, direction = momentum_of(columns, spread)
    param_step = step_of(offsets, totals, direction, dense)
    return (momentum_new.reshape(1, BUCKET), param_step.reshape(1, BUCKET))


def solution(mesh):
    split = Mesh(mesh.devices.reshape(N_Z, N_Y, N_TENSOR), ("z", "y", "tensor"))
    dp = ("z", "y")
    placed = (
        P(dp, "tensor", None),
        P(dp, "tensor", None),
        P("tensor", None),
        P("tensor", None),
        P("tensor", None),
        P("tensor", dp),
        P(),
        P(),
    )
    return jax.shard_map(
        body,
        mesh=split,
        in_specs=placed,
        out_specs=(P("tensor", None), P("tensor", None)),
        check_vma=False,
    )
```

```python
import functools

import jax
import jax.numpy as jnp
from jax import lax
from jax.experimental import pallas as pl
from jax.experimental.pallas import tpu as pltpu
from jax.sharding import Mesh, PartitionSpec as P

QB = 128
BETA_ONE = 0.9
BETA_TWO = 0.999
ADAM_EPS = 1e-08
DECAY = 0.1
CLIP_RMS = 2.0

BUCKET = 524288
SEGS = 4
N_Z = 4
N_Y = 4
N_DP = N_Z * N_Y
N_TENSOR = 16
SHARE = BUCKET // N_DP
ROWS = SHARE // QB
BLOCKS = BUCKET // QB
HALF = N_Z // 2
HALF_SHAPE = (HALF, ROWS, QB)
F32 = jnp.float32
BF16 = jnp.bfloat16
MIB = 1024 * 1024
PREPARE_LIMIT = 54
ORDER = (2, 1, 3)
LAST_ORDER = (3, 1, 2)


def on_chip(count):
    return [pl.BlockSpec(memory_space=pltpu.VMEM)] * count


def anywhere(count):
    return [pl.BlockSpec(memory_space=pl.ANY)] * count


def like(shape, dtype):
    return jax.ShapeDtypeStruct(shape, dtype)


def rows_of(values):
    return values.reshape(values.shape[-1] // QB, QB)


def call(kernel, scalars, arrays, in_specs, out_specs, out_shape, scratch=(), limit=16, aliases=None):
    return pl.pallas_call(
        kernel,
        in_specs=[pl.BlockSpec(memory_space=pltpu.SMEM)] * len(scalars) + in_specs,
        out_specs=out_specs,
        out_shape=out_shape,
        scratch_shapes=scratch,
        input_output_aliases=aliases or {},
        compiler_params=pltpu.CompilerParams(vmem_limit_bytes=limit * MIB),
    )(*scalars, *arrays)


def my_z():
    return lax.axis_index("z")


def my_y():
    return lax.axis_index("y")


def share_of(ref, block):
    return rows_of(ref[:, pl.ds(pl.multiple_of(block * SHARE, SHARE), SHARE)])


def rows_at(block):
    return pl.ds(pl.multiple_of(block * ROWS, ROWS), ROWS)


def prepare_kernel(half, grad, err, *refs):
    outs, (held_grad, held_err, sems) = refs[:N_Y], refs[N_Y:]
    y = my_y()
    width = N_Y * SHARE
    copies = []
    for s in range(HALF):
        here = pl.ds((half * HALF + s) * width, width)
        there = pl.ds(s * width, width)
        copies.append(
            (
                pltpu.make_async_copy(grad.at[:, :, here], held_grad.at[:, :, there], sems.at[0, s]),
                pltpu.make_async_copy(err.at[:, :, here], held_err.at[:, :, there], sems.at[1, s]),
            )
        )
    for pair in copies:
        for copy in pair:
            copy.start()
    for s in range(HALF):
        for copy in copies[s]:
            copy.wait()
        for k in range(N_Y):
            block = pl.ds(pl.multiple_of((s * N_Y + (y ^ k)) * SHARE, SHARE), SHARE)
            g = held_grad[0, :, block].astype(F32)
            e = held_err[0, :, block].astype(F32)
            outs[k][s] = rows_of((1.0 - BETA_ONE) * g + e).astype(BF16)


def prepare(half, grad, err):
    held = pltpu.VMEM((1, 1, BUCKET // 2), BF16)
    return call(
        functools.partial(prepare_kernel, half),
        (),
        (grad, err),
        anywhere(2),
        on_chip(N_Y),
        (like(HALF_SHAPE, BF16),) * N_Y,
        scratch=[held, held, pltpu.SemaphoreType.DMA((2, HALF))],
        limit=PREPARE_LIMIT,
    )


def reduce_y_kernel(half, *refs):
    ins, server_err, out = refs[:N_Y], refs[N_Y], refs[-1]
    mine = rows_of(server_err[...])
    z = my_z()
    for s in range(HALF):
        total = ins[0][s].astype(F32)
        for ref in ins[1:]:
            total = total + ref[s].astype(F32)
        total = total * (1.0 / N_DP) + jnp.where(z == half * HALF + s, mine, 0.0)
        out[s] = total.astype(BF16)


def reduce_y(half, pieces, server_err, *staged):
    (out,) = call(
        functools.partial(reduce_y_kernel, half),
        (),
        (*pieces, server_err, *staged),
        on_chip(N_Y + 1) + anywhere(len(staged)),
        on_chip(1),
        [like(HALF_SHAPE, BF16)],
    )
    return out


def add_kernel(ours, theirs, *refs):
    out = refs[-1]
    out[...] = (ours[...].astype(F32) + theirs[...].astype(F32)).astype(BF16)


def add(ours, theirs, *staged):
    (out,) = call(
        add_kernel,
        (),
        (ours, theirs, *staged),
        on_chip(2) + anywhere(len(staged)),
        on_chip(1),
        [like(HALF_SHAPE, BF16)],
    )
    return out


def row_masks(offsets, first_row, rows):
    entry = (first_row + lax.broadcasted_iota(jnp.int32, (rows, QB), 0)) * QB
    return [entry >= offsets[k] for k in range(1, SEGS)]


def has_boundary(offsets, first_row, rows):
    inside = [(offsets[k] > first_row * QB) & (offsets[k] < (first_row + rows) * QB) for k in range(1, SEGS)]
    return inside[0] | inside[1] | inside[2]


def server_kernel(offsets, low, high, other_low, other_high, momentum, spread, column, out, sums):
    y = my_y()
    lane_row = lax.broadcasted_iota(jnp.int32, (8, QB), 0)
    sums[...] = jnp.zeros((8, QB), F32)
    for s in range(N_Z):
        ours, theirs = (low, other_low) if s < HALF else (high, other_high)
        total = ours[s % HALF].astype(F32) + theirs[s % HALF].astype(F32)
        block = s * N_Y + y
        sent = (total + BETA_ONE * share_of(momentum, block)).astype(BF16)
        column[s] = sent
        direction = sent.astype(F32) * spread[s]
        squares = direction * direction
        first = block * ROWS
        mixed = has_boundary(offsets, first, ROWS)

        @pl.when(jnp.logical_not(mixed))
        def _(squares=squares, first=first):
            tensor = sum((first * QB >= offsets[k]).astype(jnp.int32) for k in range(1, SEGS))
            sums[...] += jnp.where(lane_row == tensor, jnp.sum(squares, axis=0, keepdims=True), 0.0)

        @pl.when(mixed)
        def _(squares=squares, first=first):
            masks = row_masks(offsets, first, ROWS)
            for k in range(SEGS):
                picked = squares
                if k > 0:
                    picked = jnp.where(masks[k - 1], picked, 0.0)
                if k < SEGS - 1:
                    picked = jnp.where(masks[k], 0.0, picked)
                sums[k : k + 1, :] += jnp.sum(picked, axis=0, keepdims=True)
    folded = sums[...]
    folded = folded + pltpu.roll(folded, QB // 2, 1)
    folded = folded + pltpu.roll(folded, QB // 4, 1)
    lane = lax.broadcasted_iota(jnp.int32, (8, QB), 1) // (QB // SEGS)
    mine = jnp.where(lane == lane_row, folded, 0.0)
    out[...] = jnp.broadcast_to(jnp.sum(mine, axis=0, keepdims=True)[None], out.shape)


def server(offsets, halves, momentum, spread):
    return call(
        server_kernel,
        (offsets,),
        (*halves, momentum, spread),
        on_chip(6),
        on_chip(2),
        (like((N_Z, ROWS, QB), BF16), like((N_Y * N_TENSOR, 1, QB), F32)),
        scratch=[pltpu.VMEM((8, QB), F32)],
    )


def spread_kernel(bias, variance, spread, column_spread):
    for block in range(N_DP):
        root = jnp.sqrt(share_of(variance, block) * bias[1]) + ADAM_EPS
        spread[block * ROWS : (block + 1) * ROWS, :] = bias[0] / root
    for s in range(N_Z):
        column_spread[s] = spread[rows_at(s * N_Y + my_y()), :]


def spread_of(bias, variance):
    return call(
        spread_kernel,
        (bias,),
        (variance,),
        on_chip(1),
        on_chip(2),
        (like((BLOCKS, QB), F32), like((N_Z, ROWS, QB), F32)),
    )


def dense_kernel(weights, out):
    for block in range(N_DP):
        out[block * ROWS : (block + 1) * ROWS, :] = share_of(weights, block).astype(BF16)


def dense_of(weights):
    (out,) = call(dense_kernel, (), (weights,), on_chip(1), on_chip(1), [like((BLOCKS, QB), BF16)])
    return out


def momentum_kernel(*refs):
    pieces, (spread, out, direction, held, sems) = refs[:N_Y], refs[N_Y:]
    y = my_y()
    stores = []
    for s in range(N_Z):
        for k, piece in zip((0, *LAST_ORDER), pieces):
            rows = rows_at(s * N_Y + (y ^ k))
            kept = piece[s].astype(F32)
            held[rows, :] = kept
            direction[rows, :] = kept * spread[rows, :]
        rows = pl.ds(s * N_Y * ROWS, N_Y * ROWS)
        stores.append(pltpu.make_async_copy(held.at[rows], out.at[rows], sems.at[s]))
        stores[-1].start()
    for store in stores:
        store.wait()


def momentum_of(pieces, spread):
    out = like((BLOCKS, QB), F32)
    return call(
        momentum_kernel,
        (),
        (*pieces, spread),
        on_chip(N_Y + 1),
        anywhere(1) + on_chip(1),
        (out, out),
        scratch=[pltpu.VMEM((BLOCKS, QB), F32), pltpu.SemaphoreType.DMA((N_Z,))],
        aliases={N_Y: 1},
    )


def step_kernel(offsets, totals, direction, dense, out, held, sems):
    total = jnp.sum(totals[...], axis=0)
    lane = lax.broadcasted_iota(jnp.int32, (1, QB), 1) // (QB // SEGS)
    inverse = []
    for k in range(SEGS):
        end = offsets[k + 1] if k + 1 < SEGS else BUCKET
        entries = (end - offsets[k]).astype(F32) * N_TENSOR
        squares = jnp.sum(jnp.where(lane == k, total, 0.0), axis=1, keepdims=True)
        inverse.append(1.0 / jnp.maximum(1.0, jnp.sqrt(squares / entries + 1e-06) / CLIP_RMS))
    copies = []
    for part in range(BLOCKS // ROWS):
        first = part * ROWS
        rows = pl.ds(first, ROWS)
        mixed = has_boundary(offsets, first, ROWS)

        @pl.when(jnp.logical_not(mixed))
        def _(rows=rows, first=first):
            factor = inverse[0]
            for k in range(1, SEGS):
                factor = jnp.where(first * QB >= offsets[k], inverse[k], factor)
            held[rows, :] = direction[rows, :] * factor + DECAY * dense[rows, :].astype(F32)

        @pl.when(mixed)
        def _(rows=rows, first=first):
            factor = jnp.broadcast_to(inverse[0], (ROWS, QB))
            for k, mask in enumerate(row_masks(offsets, first, ROWS)):
                factor = jnp.where(mask, inverse[k + 1], factor)
            held[rows, :] = direction[rows, :] * factor + DECAY * dense[rows, :].astype(F32)

        copies.append(pltpu.make_async_copy(held.at[rows], out.at[rows], sems.at[part]))
        copies[-1].start()
    for copy in copies:
        copy.wait()


def step_of(offsets, totals, direction, dense):
    (out,) = call(
        step_kernel,
        (offsets,),
        (totals, direction, dense),
        on_chip(3),
        anywhere(1),
        [like((BLOCKS, QB), F32)],
        scratch=[pltpu.VMEM((BLOCKS, QB), F32), pltpu.SemaphoreType.DMA((BLOCKS // ROWS,))],
    )
    return out


def exchange(value, axis, mask):
    return lax.ppermute(value, axis, [(i, i ^ mask) for i in range(lax.axis_size(axis))])


def exchange_z(value, even, odd):
    pairs = [
        (z * N_TENSOR + t, (z ^ (odd if t % 2 else even)) * N_TENSOR + t)
        for z in range(N_Z)
        for t in range(N_TENSOR)
    ]
    return lax.ppermute(value, ("z", "tensor"), pairs)


def body(grad, worker_err, momentum, variance, params, server_err, offsets, step_count):
    steps = step_count[0].astype(F32)
    first = 1.0 - jnp.power(F32(BETA_ONE), steps)
    second = 1.0 - jnp.power(F32(BETA_TWO), steps)
    bias = jnp.stack([1.0 / first, 1.0 / second])

    spread, column_spread = spread_of(bias, variance)
    dense = dense_of(params)
    low_y, high_y = prepare(0, grad, worker_err), prepare(1, grad, worker_err)
    low = [low_y[0]] + [exchange(low_y[k], "y", k) for k in ORDER]
    high = [high_y[0]] + [exchange(high_y[k], "y", k) for k in ORDER]
    low = reduce_y(0, low, server_err)
    high = reduce_y(1, high, server_err, dense)
    low = add(low, exchange_z(low, 1, 3))
    high = add(high, exchange_z(high, 3, 1))
    halves = (low, high, exchange_z(low, 3, 1), exchange_z(high, 1, 3))
    column, squares = server(offsets, halves, momentum, column_spread)
    columns = [column] + [exchange(column, "y", k) for k in LAST_ORDER]
    totals = lax.all_to_all(squares, ("y", "tensor"), split_axis=0, concat_axis=0, tiled=True)
    momentum_new, direction = momentum_of(columns, spread)
    param_step = step_of(offsets, totals, direction, dense)
    return (momentum_new.reshape(1, BUCKET), param_step.reshape(1, BUCKET))


def solution(mesh):
    split = Mesh(mesh.devices.reshape(N_Z, N_Y, N_TENSOR), ("z", "y", "tensor"))
    dp = ("z", "y")
    placed = (
        P(dp, "tensor", None),
        P(dp, "tensor", None),
        P("tensor", None),
        P("tensor", None),
        P("tensor", None),
        P("tensor", dp),
        P(),
        P(),
    )
    return jax.shard_map(
        body,
        mesh=split,
        in_specs=placed,
        out_specs=(P("tensor", None), P("tensor", None)),
        check_vma=False,
    )
```

```python
import functools

import jax
import jax.numpy as jnp
from jax import lax
from jax.experimental import pallas as pl
from jax.experimental.pallas import tpu as pltpu
from jax.sharding import Mesh, PartitionSpec as P

QB = 128
BETA_ONE = 0.9
BETA_TWO = 0.999
ADAM_EPS = 1e-08
DECAY = 0.1
CLIP_RMS = 2.0

BUCKET = 524288
SEGS = 4
N_Z = 4
N_Y = 4
N_DP = N_Z * N_Y
N_TENSOR = 16
N_CORE = 2
N_CHIP = N_TENSOR // N_CORE
SHARE = BUCKET // N_DP
ROWS = SHARE // QB
BLOCKS = BUCKET // QB
HALF = N_Z // 2
HALF_SHAPE = (HALF, ROWS, QB)
F32 = jnp.float32
BF16 = jnp.bfloat16
MIB = 1024 * 1024
PREPARE_LIMIT = 54
ORDER = (2, 1, 3)
EARLY, LATE = (0, 2), (1, 3)
GATHER = (2, 1, 3)


def on_chip(count):
    return [pl.BlockSpec(memory_space=pltpu.VMEM)] * count


def anywhere(count):
    return [pl.BlockSpec(memory_space=pl.ANY)] * count


def like(shape, dtype):
    return jax.ShapeDtypeStruct(shape, dtype)


def rows_of(values):
    return values.reshape(values.shape[-1] // QB, QB)


def call(kernel, scalars, arrays, in_specs, out_specs, out_shape, scratch=(), limit=16, aliases=None):
    return pl.pallas_call(
        kernel,
        in_specs=[pl.BlockSpec(memory_space=pltpu.SMEM)] * len(scalars) + in_specs,
        out_specs=out_specs,
        out_shape=out_shape,
        scratch_shapes=scratch,
        input_output_aliases=aliases or {},
        compiler_params=pltpu.CompilerParams(vmem_limit_bytes=limit * MIB),
    )(*scalars, *arrays)


def my_z():
    return lax.axis_index("z")


def my_y():
    return lax.axis_index("y")


def partner(y, k):
    return y ^ k ^ (2 * lax.axis_index("core")) if k % 2 else y ^ k


def share_of(ref, block):
    return rows_of(ref[:, pl.ds(pl.multiple_of(block * SHARE, SHARE), SHARE)])


def rows_at(block):
    return pl.ds(pl.multiple_of(block * ROWS, ROWS), ROWS)


def prepare_kernel(half, grad, err, *refs):
    outs, (held_grad, held_err, held_out, sems, out_sems) = refs[:N_Y], refs[N_Y:]
    y = my_y()
    width = N_Y * SHARE
    copies = []
    for s in range(HALF):
        here = pl.ds((half * HALF + s) * width, width)
        there = pl.ds(s * width, width)
        copies.append(
            (
                pltpu.make_async_copy(grad.at[:, :, here], held_grad.at[:, :, there], sems.at[0, s]),
                pltpu.make_async_copy(err.at[:, :, here], held_err.at[:, :, there], sems.at[1, s]),
            )
        )
    for pair in copies:
        for copy in pair:
            copy.start()
    stores = []
    for s in range(HALF):
        for copy in copies[s]:
            copy.wait()
        for k in range(N_Y):
            block = pl.ds(pl.multiple_of((s * N_Y + partner(y, k)) * SHARE, SHARE), SHARE)
            g = held_grad[0, :, block].astype(F32)
            e = held_err[0, :, block].astype(F32)
            held_out[k, s] = rows_of((1.0 - BETA_ONE) * g + e).astype(BF16)
            stores.append(pltpu.make_async_copy(held_out.at[k, s], outs[k].at[s], out_sems.at[k, s]))
            stores[-1].start()
    for store in stores:
        store.wait()


def prepare(half, grad, err):
    held = pltpu.VMEM((1, 1, BUCKET // 2), BF16)
    return call(
        functools.partial(prepare_kernel, half),
        (),
        (grad, err),
        anywhere(2),
        anywhere(N_Y),
        (like(HALF_SHAPE, BF16),) * N_Y,
        scratch=[
            held,
            held,
            pltpu.VMEM((N_Y, *HALF_SHAPE), BF16),
            pltpu.SemaphoreType.DMA((2, HALF)),
            pltpu.SemaphoreType.DMA((N_Y, HALF)),
        ],
        limit=PREPARE_LIMIT,
    )


def reduce_y_kernel(half, *refs):
    ins, server_err, out = refs[:N_Y], refs[N_Y], refs[-1]
    mine = rows_of(server_err[...])
    z = my_z()
    for s in range(HALF):
        total = ins[0][s].astype(F32)
        for ref in ins[1:]:
            total = total + ref[s].astype(F32)
        total = total * (1.0 / N_DP) + jnp.where(z == half * HALF + s, mine, 0.0)
        out[s] = total.astype(BF16)


def reduce_y(half, pieces, server_err, *staged):
    (out,) = call(
        functools.partial(reduce_y_kernel, half),
        (),
        (*pieces, server_err, *staged),
        on_chip(N_Y + 1) + anywhere(len(staged)),
        on_chip(1),
        [like(HALF_SHAPE, BF16)],
    )
    return out


def add_kernel(ours, theirs, *refs):
    out = refs[-1]
    out[...] = (ours[...].astype(F32) + theirs[...].astype(F32)).astype(BF16)


def add(ours, theirs, *staged):
    (out,) = call(
        add_kernel,
        (),
        (ours, theirs, *staged),
        on_chip(2) + anywhere(len(staged)),
        on_chip(1),
        [like(HALF_SHAPE, BF16)],
    )
    return out


def row_masks(offsets, first_row, rows):
    entry = (first_row + lax.broadcasted_iota(jnp.int32, (rows, QB), 0)) * QB
    return [entry >= offsets[k] for k in range(1, SEGS)]


def has_boundary(offsets, first_row, rows):
    inside = [(offsets[k] > first_row * QB) & (offsets[k] < (first_row + rows) * QB) for k in range(1, SEGS)]
    return inside[0] | inside[1] | inside[2]


def server_kernel(offsets, low, high, other_low, other_high, momentum, spread, column, out, sums):
    y = my_y()
    lane_row = lax.broadcasted_iota(jnp.int32, (8, QB), 0)
    sums[...] = jnp.zeros((8, QB), F32)
    for s in range(N_Z):
        ours, theirs = (low, other_low) if s < HALF else (high, other_high)
        total = ours[s % HALF].astype(F32) + theirs[s % HALF].astype(F32)
        block = s * N_Y + y
        sent = (total + BETA_ONE * share_of(momentum, block)).astype(BF16)
        column[s] = sent
        direction = sent.astype(F32) * spread[s]
        squares = direction * direction
        first = block * ROWS
        mixed = has_boundary(offsets, first, ROWS)

        @pl.when(jnp.logical_not(mixed))
        def _(squares=squares, first=first):
            tensor = sum((first * QB >= offsets[k]).astype(jnp.int32) for k in range(1, SEGS))
            sums[...] += jnp.where(lane_row == tensor, jnp.sum(squares, axis=0, keepdims=True), 0.0)

        @pl.when(mixed)
        def _(squares=squares, first=first):
            masks = row_masks(offsets, first, ROWS)
            for k in range(SEGS):
                picked = squares
                if k > 0:
                    picked = jnp.where(masks[k - 1], picked, 0.0)
                if k < SEGS - 1:
                    picked = jnp.where(masks[k], 0.0, picked)
                sums[k : k + 1, :] += jnp.sum(picked, axis=0, keepdims=True)
    folded = sums[...]
    folded = folded + pltpu.roll(folded, QB // 2, 1)
    folded = folded + pltpu.roll(folded, QB // 4, 1)
    lane = lax.broadcasted_iota(jnp.int32, (8, QB), 1) // (QB // SEGS)
    mine = jnp.where(lane == lane_row, folded, 0.0)
    out[...] = jnp.broadcast_to(jnp.sum(mine, axis=0, keepdims=True), out.shape)


def server(offsets, halves, momentum, spread):
    return call(
        server_kernel,
        (offsets,),
        (*halves, momentum, spread),
        on_chip(6),
        on_chip(2),
        (like((N_Z, ROWS, QB), BF16), like((512, QB), F32)),
        scratch=[pltpu.VMEM((8, QB), F32)],
    )


def pair_kernel(ours, theirs, out):
    out[...] = jnp.broadcast_to((ours[:1, :] + theirs[:1, :])[None], out.shape)


def pair(ours, theirs):
    (out,) = call(
        pair_kernel, (), (ours, theirs), on_chip(2), on_chip(1), [like((N_Y * N_CHIP, 1, QB), F32)]
    )
    return out


def spread_kernel(bias, variance, spread, column_spread):
    for block in range(N_DP):
        root = jnp.sqrt(share_of(variance, block) * bias[1]) + ADAM_EPS
        spread[block * ROWS : (block + 1) * ROWS, :] = bias[0] / root
    for s in range(N_Z):
        column_spread[s] = spread[rows_at(s * N_Y + my_y()), :]


def spread_of(bias, variance):
    return call(
        spread_kernel,
        (bias,),
        (variance,),
        on_chip(1),
        on_chip(2),
        (like((BLOCKS, QB), F32), like((N_Z, ROWS, QB), F32)),
    )


def dense_kernel(weights, out):
    for block in range(N_DP):
        out[block * ROWS : (block + 1) * ROWS, :] = share_of(weights, block).astype(BF16)


def dense_of(weights):
    (out,) = call(dense_kernel, (), (weights,), on_chip(1), on_chip(1), [like((BLOCKS, QB), BF16)])
    return out


def momentum_kernel(ks, *refs):
    pieces = refs[: len(ks)]
    out, direction, held, sems = refs[-4:]
    y = my_y()
    stores = []
    for s in range(N_Z):
        for j, (k, piece) in enumerate(zip(ks, pieces)):
            rows = rows_at(s * N_Y + partner(y, k))
            kept = piece[s].astype(F32)
            held[j, s] = kept
            direction[rows, :] = kept * direction[rows, :]
            stores.append(pltpu.make_async_copy(held.at[j, s], out.at[rows], sems.at[j, s]))
            stores[-1].start()
    for store in stores:
        store.wait()


def momentum_of(ks, pieces, spread, *partial):
    out = like((BLOCKS, QB), F32)
    count = len(ks)
    aliases = {count: 1}
    if partial:
        aliases[count + 1] = 0
    return call(
        functools.partial(momentum_kernel, ks),
        (),
        (*pieces, spread, *partial),
        on_chip(count + 1) + anywhere(len(partial)),
        anywhere(1) + on_chip(1),
        (out, out),
        scratch=[pltpu.VMEM((count, N_Z, ROWS, QB), F32), pltpu.SemaphoreType.DMA((count, N_Z))],
        aliases=aliases,
    )


def step_kernel(offsets, totals, direction, dense, out, held, sems):
    total = jnp.sum(totals[...], axis=0)
    lane = lax.broadcasted_iota(jnp.int32, (1, QB), 1) // (QB // SEGS)
    inverse = []
    for k in range(SEGS):
        end = offsets[k + 1] if k + 1 < SEGS else BUCKET
        entries = (end - offsets[k]).astype(F32) * N_TENSOR
        squares = jnp.sum(jnp.where(lane == k, total, 0.0), axis=1, keepdims=True)
        inverse.append(1.0 / jnp.maximum(1.0, jnp.sqrt(squares / entries + 1e-06) / CLIP_RMS))
    stores = []
    for block in range(N_DP):
        first = block * ROWS
        rows = pl.ds(first, ROWS)
        mixed = has_boundary(offsets, first, ROWS)

        @pl.when(jnp.logical_not(mixed))
        def _(rows=rows, first=first):
            factor = inverse[0]
            for k in range(1, SEGS):
                factor = jnp.where(first * QB >= offsets[k], inverse[k], factor)
            held[rows, :] = direction[rows, :] * factor + DECAY * dense[rows, :].astype(F32)

        @pl.when(mixed)
        def _(rows=rows, first=first):
            factor = jnp.broadcast_to(inverse[0], (ROWS, QB))
            for k, mask in enumerate(row_masks(offsets, first, ROWS)):
                factor = jnp.where(mask, inverse[k + 1], factor)
            held[rows, :] = direction[rows, :] * factor + DECAY * dense[rows, :].astype(F32)

        stores.append(pltpu.make_async_copy(held.at[rows], out.at[rows], sems.at[block]))
        stores[-1].start()
    for store in stores:
        store.wait()


def step_of(offsets, totals, direction, dense):
    (out,) = call(
        step_kernel,
        (offsets,),
        (totals, direction, dense),
        on_chip(3),
        anywhere(1),
        [like((BLOCKS, QB), F32)],
        scratch=[pltpu.VMEM((BLOCKS, QB), F32), pltpu.SemaphoreType.DMA((N_DP,))],
    )
    return out


def exchange(value, axis, mask):
    return lax.ppermute(value, axis, [(i, i ^ mask) for i in range(lax.axis_size(axis))])


def exchange_y(value, k):
    pairs = []
    for y in range(N_Y):
        for t in range(N_TENSOR):
            to = y ^ k ^ (2 * (t % N_CORE) if k % 2 else 0)
            pairs.append((y * N_TENSOR + t, to * N_TENSOR + t))
    return lax.ppermute(value, ("y", "chip", "core"), pairs)


def exchange_z(value, even, odd):
    pairs = [
        (z * N_TENSOR + t, (z ^ (odd if t % 2 else even)) * N_TENSOR + t)
        for z in range(N_Z)
        for t in range(N_TENSOR)
    ]
    return lax.ppermute(value, ("z", "chip", "core"), pairs)


def body(grad, worker_err, momentum, variance, params, server_err, offsets, step_count):
    steps = step_count[0].astype(F32)
    first = 1.0 - jnp.power(F32(BETA_ONE), steps)
    second = 1.0 - jnp.power(F32(BETA_TWO), steps)
    bias = jnp.stack([1.0 / first, 1.0 / second])

    spread, column_spread = spread_of(bias, variance)
    dense = dense_of(params)
    low_y, high_y = prepare(0, grad, worker_err), prepare(1, grad, worker_err)
    low = [low_y[0]] + [exchange_y(low_y[k], k) for k in ORDER]
    high = [high_y[0]] + [exchange_y(high_y[k], k) for k in ORDER]
    low = reduce_y(0, low, server_err)
    high = reduce_y(1, high, server_err, dense)
    low = add(low, exchange_z(low, 3, 1))
    high = add(high, exchange_z(high, 1, 3))
    halves = (low, high, exchange_z(low, 1, 3), exchange_z(high, 3, 1))
    column, squares = server(offsets, halves, momentum, column_spread)
    received = {k: exchange_y(column, k) for k in GATHER}
    squares = pair(squares, exchange(squares, "core", 1))
    totals = lax.all_to_all(squares, ("y", "chip"), split_axis=0, concat_axis=0, tiled=True)
    partial, direction = momentum_of(EARLY, [column] + [received[k] for k in EARLY[1:]], spread)
    momentum_new, direction = momentum_of(LATE, [received[k] for k in LATE], direction, partial)
    param_step = step_of(offsets, totals, direction, dense)
    return (momentum_new.reshape(1, BUCKET), param_step.reshape(1, BUCKET))


def solution(mesh):
    split = Mesh(mesh.devices.reshape(N_Z, N_Y, N_CHIP, N_CORE), ("z", "y", "chip", "core"))
    dp, tensor = ("z", "y"), ("chip", "core")
    placed = (
        P(dp, tensor, None),
        P(dp, tensor, None),
        P(tensor, None),
        P(tensor, None),
        P(tensor, None),
        P(tensor, dp),
        P(),
        P(),
    )
    return jax.shard_map(
        body,
        mesh=split,
        in_specs=placed,
        out_specs=(P(tensor, None), P(tensor, None)),
        check_vma=False,
    )
```

```python
import functools

import jax
import jax.numpy as jnp
from jax import lax
from jax.experimental import pallas as pl
from jax.experimental.pallas import tpu as pltpu
from jax.sharding import Mesh, PartitionSpec as P

QB = 128
BETA_ONE = 0.9
BETA_TWO = 0.999
ADAM_EPS = 1e-08
DECAY = 0.1
CLIP_RMS = 2.0

BUCKET = 524288
SEGS = 4
N_Z = 4
N_Y = 4
N_DP = N_Z * N_Y
N_TENSOR = 16
N_CORE = 2
N_CHIP = N_TENSOR // N_CORE
SHARE = BUCKET // N_DP
ROWS = SHARE // QB
BLOCKS = BUCKET // QB
HALF = N_Z // 2
HALF_SHAPE = (HALF, ROWS, QB)
F32 = jnp.float32
BF16 = jnp.bfloat16
MIB = 1024 * 1024
PREPARE_LIMIT = 54
ORDER = (2, 1, 3)
EARLY, LATE = (0, 2), (1, 3)
GATHER = (2, 1, 3)


def on_chip(count):
    return [pl.BlockSpec(memory_space=pltpu.VMEM)] * count


def anywhere(count):
    return [pl.BlockSpec(memory_space=pl.ANY)] * count


def like(shape, dtype):
    return jax.ShapeDtypeStruct(shape, dtype)


def rows_of(values):
    return values.reshape(values.shape[-1] // QB, QB)


def call(kernel, scalars, arrays, in_specs, out_specs, out_shape, scratch=(), limit=16, aliases=None):
    return pl.pallas_call(
        kernel,
        in_specs=[pl.BlockSpec(memory_space=pltpu.SMEM)] * len(scalars) + in_specs,
        out_specs=out_specs,
        out_shape=out_shape,
        scratch_shapes=scratch,
        input_output_aliases=aliases or {},
        compiler_params=pltpu.CompilerParams(vmem_limit_bytes=limit * MIB),
    )(*scalars, *arrays)


def my_z():
    return lax.axis_index("z")


def my_y():
    return lax.axis_index("y")


def partner(y, k):
    return y ^ k ^ (2 * lax.axis_index("core")) if k % 2 else y ^ k


def share_of(ref, block):
    return rows_of(ref[:, pl.ds(pl.multiple_of(block * SHARE, SHARE), SHARE)])


def rows_at(block):
    return pl.ds(pl.multiple_of(block * ROWS, ROWS), ROWS)


def prepare_kernel(half, grad, err, *refs):
    outs, (held_grad, held_err, held_out, sems, out_sems) = refs[:N_Y], refs[N_Y:]
    y = my_y()
    width = N_Y * SHARE
    copies = []
    for s in range(HALF):
        here = pl.ds((half * HALF + s) * width, width)
        there = pl.ds(s * width, width)
        copies.append(
            (
                pltpu.make_async_copy(grad.at[:, :, here], held_grad.at[:, :, there], sems.at[0, s]),
                pltpu.make_async_copy(err.at[:, :, here], held_err.at[:, :, there], sems.at[1, s]),
            )
        )
    for pair in copies:
        for copy in pair:
            copy.start()
    stores = []
    for s in range(HALF):
        for copy in copies[s]:
            copy.wait()
        for k in range(N_Y):
            block = pl.ds(pl.multiple_of((s * N_Y + partner(y, k)) * SHARE, SHARE), SHARE)
            g = held_grad[0, :, block].astype(F32)
            e = held_err[0, :, block].astype(F32)
            held_out[k, s] = rows_of((1.0 - BETA_ONE) * g + e).astype(BF16)
            stores.append(pltpu.make_async_copy(held_out.at[k, s], outs[k].at[s], out_sems.at[k, s]))
            stores[-1].start()
    for store in stores:
        store.wait()


def prepare(half, grad, err):
    held = pltpu.VMEM((1, 1, BUCKET // 2), BF16)
    return call(
        functools.partial(prepare_kernel, half),
        (),
        (grad, err),
        anywhere(2),
        anywhere(N_Y),
        (like(HALF_SHAPE, BF16),) * N_Y,
        scratch=[
            held,
            held,
            pltpu.VMEM((N_Y, *HALF_SHAPE), BF16),
            pltpu.SemaphoreType.DMA((2, HALF)),
            pltpu.SemaphoreType.DMA((N_Y, HALF)),
        ],
        limit=PREPARE_LIMIT,
    )


def reduce_y_kernel(half, *refs):
    ins, server_err, out = refs[:N_Y], refs[N_Y], refs[-1]
    mine = rows_of(server_err[...])
    z = my_z()
    for s in range(HALF):
        total = ins[0][s].astype(F32)
        for ref in ins[1:]:
            total = total + ref[s].astype(F32)
        total = total * (1.0 / N_DP) + jnp.where(z == half * HALF + s, mine, 0.0)
        out[s] = total.astype(BF16)


def reduce_y(half, pieces, server_err, *staged):
    (out,) = call(
        functools.partial(reduce_y_kernel, half),
        (),
        (*pieces, server_err, *staged),
        on_chip(N_Y + 1) + anywhere(len(staged)),
        on_chip(1),
        [like(HALF_SHAPE, BF16)],
    )
    return out


def add_kernel(ours, theirs, *refs):
    out = refs[-1]
    out[...] = (ours[...].astype(F32) + theirs[...].astype(F32)).astype(BF16)


def add(ours, theirs, *staged):
    (out,) = call(
        add_kernel,
        (),
        (ours, theirs, *staged),
        on_chip(2) + anywhere(len(staged)),
        on_chip(1),
        [like(HALF_SHAPE, BF16)],
    )
    return out


def row_masks(offsets, first_row, rows):
    entry = (first_row + lax.broadcasted_iota(jnp.int32, (rows, QB), 0)) * QB
    return [entry >= offsets[k] for k in range(1, SEGS)]


def has_boundary(offsets, first_row, rows):
    inside = [(offsets[k] > first_row * QB) & (offsets[k] < (first_row + rows) * QB) for k in range(1, SEGS)]
    return inside[0] | inside[1] | inside[2]


def server_kernel(half, offsets, ours, theirs, momentum, spread, *refs):
    column, sums = refs[-2:] if half == 0 else (refs[2], refs[4])
    y = my_y()
    lane_row = lax.broadcasted_iota(jnp.int32, (8, QB), 0)
    sums[...] = jnp.zeros((8, QB), F32) if half == 0 else refs[0][...]
    for s in range(HALF):
        block = (half * HALF + s) * N_Y + y
        total = ours[s].astype(F32) + theirs[s].astype(F32)
        sent = (total + BETA_ONE * share_of(momentum, block)).astype(BF16)
        column[half * HALF + s] = sent
        direction = sent.astype(F32) * spread[half * HALF + s]
        squares = direction * direction
        first = block * ROWS
        mixed = has_boundary(offsets, first, ROWS)

        @pl.when(jnp.logical_not(mixed))
        def _(squares=squares, first=first):
            tensor = sum((first * QB >= offsets[k]).astype(jnp.int32) for k in range(1, SEGS))
            sums[...] += jnp.where(lane_row == tensor, jnp.sum(squares, axis=0, keepdims=True), 0.0)

        @pl.when(mixed)
        def _(squares=squares, first=first):
            masks = row_masks(offsets, first, ROWS)
            for k in range(SEGS):
                picked = squares
                if k > 0:
                    picked = jnp.where(masks[k - 1], picked, 0.0)
                if k < SEGS - 1:
                    picked = jnp.where(masks[k], 0.0, picked)
                sums[k : k + 1, :] += jnp.sum(picked, axis=0, keepdims=True)

    if half == 1:
        out = refs[3]
        folded = sums[...]
        folded = folded + pltpu.roll(folded, QB // 2, 1)
        folded = folded + pltpu.roll(folded, QB // 4, 1)
        lane = lax.broadcasted_iota(jnp.int32, (8, QB), 1) // (QB // SEGS)
        mine = jnp.where(lane == lane_row, folded, 0.0)
        out[...] = jnp.broadcast_to(jnp.sum(mine, axis=0, keepdims=True), out.shape)


def server(half, offsets, ours, theirs, momentum, spread, *before):
    return call(
        functools.partial(server_kernel, half),
        (offsets,),
        (ours, theirs, momentum, spread, *before),
        on_chip(4 + len(before)),
        on_chip(2),
        (like((N_Z, ROWS, QB), BF16), like((512 if half else 8, QB), F32)),
        scratch=[pltpu.VMEM((8, QB), F32)] * half,
        aliases={6: 0} if half else None,
    )


def pair_kernel(ours, theirs, out):
    out[...] = jnp.broadcast_to((ours[:1, :] + theirs[:1, :])[None], out.shape)


def pair(ours, theirs):
    (out,) = call(
        pair_kernel, (), (ours, theirs), on_chip(2), on_chip(1), [like((N_Y * N_CHIP, 1, QB), F32)]
    )
    return out


def spread_kernel(bias, variance, spread, column_spread):
    for block in range(N_DP):
        root = jnp.sqrt(share_of(variance, block) * bias[1]) + ADAM_EPS
        spread[block * ROWS : (block + 1) * ROWS, :] = bias[0] / root
    for s in range(N_Z):
        column_spread[s] = spread[rows_at(s * N_Y + my_y()), :]


def spread_of(bias, variance):
    return call(
        spread_kernel,
        (bias,),
        (variance,),
        on_chip(1),
        on_chip(2),
        (like((BLOCKS, QB), F32), like((N_Z, ROWS, QB), F32)),
    )


def dense_kernel(weights, out):
    for block in range(N_DP):
        out[block * ROWS : (block + 1) * ROWS, :] = share_of(weights, block).astype(BF16)


def dense_of(weights):
    (out,) = call(dense_kernel, (), (weights,), on_chip(1), on_chip(1), [like((BLOCKS, QB), BF16)])
    return out


def momentum_kernel(ks, *refs):
    pieces = refs[: len(ks)]
    out, direction, held, sems = refs[-4:]
    y = my_y()
    stores = []
    for s in range(N_Z):
        for j, (k, piece) in enumerate(zip(ks, pieces)):
            rows = rows_at(s * N_Y + partner(y, k))
            kept = piece[s].astype(F32)
            held[j, s] = kept
            direction[rows, :] = kept * direction[rows, :]
            stores.append(pltpu.make_async_copy(held.at[j, s], out.at[rows], sems.at[j, s]))
            stores[-1].start()
    for store in stores:
        store.wait()


def momentum_of(ks, pieces, spread, *partial):
    out = like((BLOCKS, QB), F32)
    count = len(ks)
    aliases = {count: 1}
    if partial:
        aliases[count + 1] = 0
    return call(
        functools.partial(momentum_kernel, ks),
        (),
        (*pieces, spread, *partial),
        on_chip(count + 1) + anywhere(len(partial)),
        anywhere(1) + on_chip(1),
        (out, out),
        scratch=[pltpu.VMEM((count, N_Z, ROWS, QB), F32), pltpu.SemaphoreType.DMA((count, N_Z))],
        aliases=aliases,
    )


def step_kernel(offsets, totals, direction, dense, out, held, sems):
    total = jnp.sum(totals[...], axis=0)
    lane = lax.broadcasted_iota(jnp.int32, (1, QB), 1) // (QB // SEGS)
    inverse = []
    for k in range(SEGS):
        end = offsets[k + 1] if k + 1 < SEGS else BUCKET
        entries = (end - offsets[k]).astype(F32) * N_TENSOR
        squares = jnp.sum(jnp.where(lane == k, total, 0.0), axis=1, keepdims=True)
        inverse.append(1.0 / jnp.maximum(1.0, jnp.sqrt(squares / entries + 1e-06) / CLIP_RMS))
    stores = []
    for block in range(N_DP):
        first = block * ROWS
        rows = pl.ds(first, ROWS)
        mixed = has_boundary(offsets, first, ROWS)

        @pl.when(jnp.logical_not(mixed))
        def _(rows=rows, first=first):
            factor = inverse[0]
            for k in range(1, SEGS):
                factor = jnp.where(first * QB >= offsets[k], inverse[k], factor)
            held[rows, :] = direction[rows, :] * factor + DECAY * dense[rows, :].astype(F32)

        @pl.when(mixed)
        def _(rows=rows, first=first):
            factor = jnp.broadcast_to(inverse[0], (ROWS, QB))
            for k, mask in enumerate(row_masks(offsets, first, ROWS)):
                factor = jnp.where(mask, inverse[k + 1], factor)
            held[rows, :] = direction[rows, :] * factor + DECAY * dense[rows, :].astype(F32)

        stores.append(pltpu.make_async_copy(held.at[rows], out.at[rows], sems.at[block]))
        stores[-1].start()
    for store in stores:
        store.wait()


def step_of(offsets, totals, direction, dense):
    (out,) = call(
        step_kernel,
        (offsets,),
        (totals, direction, dense),
        on_chip(3),
        anywhere(1),
        [like((BLOCKS, QB), F32)],
        scratch=[pltpu.VMEM((BLOCKS, QB), F32), pltpu.SemaphoreType.DMA((N_DP,))],
    )
    return out


def exchange(value, axis, mask):
    return lax.ppermute(value, axis, [(i, i ^ mask) for i in range(lax.axis_size(axis))])


def exchange_y(value, k):
    pairs = []
    for y in range(N_Y):
        for t in range(N_TENSOR):
            to = y ^ k ^ (2 * (t % N_CORE) if k % 2 else 0)
            pairs.append((y * N_TENSOR + t, to * N_TENSOR + t))
    return lax.ppermute(value, ("y", "chip", "core"), pairs)


def exchange_z(value, even, odd):
    pairs = [
        (z * N_TENSOR + t, (z ^ (odd if t % 2 else even)) * N_TENSOR + t)
        for z in range(N_Z)
        for t in range(N_TENSOR)
    ]
    return lax.ppermute(value, ("z", "chip", "core"), pairs)


def body(grad, worker_err, momentum, variance, params, server_err, offsets, step_count):
    steps = step_count[0].astype(F32)
    first = 1.0 - jnp.power(F32(BETA_ONE), steps)
    second = 1.0 - jnp.power(F32(BETA_TWO), steps)
    bias = jnp.stack([1.0 / first, 1.0 / second])

    spread, column_spread = spread_of(bias, variance)
    dense = dense_of(params)
    low_y, high_y = prepare(0, grad, worker_err), prepare(1, grad, worker_err)
    low = [low_y[0]] + [exchange_y(low_y[k], k) for k in ORDER]
    high = [high_y[0]] + [exchange_y(high_y[k], k) for k in ORDER]
    low = reduce_y(0, low, server_err)
    high = reduce_y(1, high, server_err, dense)
    low = add(low, exchange_z(low, 3, 1))
    high = add(high, exchange_z(high, 1, 3))
    column, sums = server(0, offsets, low, exchange_z(low, 1, 3), momentum, column_spread)
    theirs = exchange_z(high, 3, 1)
    column, squares = server(1, offsets, high, theirs, momentum, column_spread, sums, column)
    received = {k: exchange_y(column, k) for k in GATHER}
    squares = pair(squares, exchange(squares, "core", 1))
    totals = lax.all_to_all(squares, ("y", "chip"), split_axis=0, concat_axis=0, tiled=True)
    partial, direction = momentum_of(EARLY, [column] + [received[k] for k in EARLY[1:]], spread)
    momentum_new, direction = momentum_of(LATE, [received[k] for k in LATE], direction, partial)
    param_step = step_of(offsets, totals, direction, dense)
    return (momentum_new.reshape(1, BUCKET), param_step.reshape(1, BUCKET))


def solution(mesh):
    split = Mesh(mesh.devices.reshape(N_Z, N_Y, N_CHIP, N_CORE), ("z", "y", "chip", "core"))
    dp, tensor = ("z", "y"), ("chip", "core")
    placed = (
        P(dp, tensor, None),
        P(dp, tensor, None),
        P(tensor, None),
        P(tensor, None),
        P(tensor, None),
        P(tensor, dp),
        P(),
        P(),
    )
    return jax.shard_map(
        body,
        mesh=split,
        in_specs=placed,
        out_specs=(P(tensor, None), P(tensor, None)),
        check_vma=False,
    )
```
